512 devices in a mesh: space: 64 (over y, z_hi, core), chan: 8 (over x, z_lo).
Axes of the slice: x: 4, y: 8, z: 8 (z_hi: 4, z_lo: 2; z = z_hi * 2 + z_lo), core: 2. Of those that a mesh axis runs over, the one named last changes fastest.
Arguments:
- blocks: bfloat16 [512, 4, 4, 4, 128], P(('space', 'chan')), may hold values from -6 to 6
- kernel_one: bfloat16 [3, 3, 3, 128, 256], replicated, may hold values from -0.109375 to 0.109375
- bias_one: float32 [256], replicated, may hold values from -3 to 3
- kernel_two: bfloat16 [3, 3, 3, 256, 256], P(None, None, None, None, 'chan'), may hold values from -0.078125 to 0.078125
- bias_two: float32 [256], P('chan'), may hold values from -3 to 3
Outputs:
- features: bfloat16 [64, 8, 8, 8, 256], P('space', None, None, None, 'chan')
The draws below stay inside these ranges and needn't reach their ends.
All inputs are finite; a program needn't handle non-finite values.
Results may differ from the reference program's by a relative error of at most 0.0045.
Values may be sent and summed in bfloat16 or wider, within the bound.
A program may use at most 64 MiB of HBM per device.

```python
import jax
import jax.numpy as jnp
from jax import lax

TILE = 8
CIN = 128
F1 = 256
F2 = 256
GY = 4
GZ = 4
GX = 4
HALF = 4
NX = 32
NY = 32
NZ = 32
N_SPACE = 64


def levels(key, extent, cuts, smallest, high):
    def one(axis_at, parts):
        heights = jax.random.uniform(jax.random.fold_in(jax.random.fold_in(key, 6), axis_at), (parts,), jnp.float32, smallest / len(cuts), high / len(cuts))
        return jnp.repeat(jnp.exp(heights), extent[axis_at] // parts).reshape((-1,) + (1,) * (len(extent) - axis_at - 1))

    loudness = one(*cuts[0])
    for cut in cuts[1:]:
        loudness = loudness * one(*cut)
    return loudness


def bell_draw(own_key, dims, deviation, bound, shards=(), kind=jnp.bfloat16):
    gain = levels(own_key, dims, shards, -0.22, 0.18) if shards else 1.0
    drawn = jax.random.normal(own_key, dims, jnp.float32) * deviation * gain
    return jnp.minimum(jnp.maximum(drawn, -bound), bound).astype(kind)


def setup_inputs(seed: int = 0) -> dict:
    seeds = jax.random.split(jax.random.key(seed), 6)
    return {
        "blocks": bell_draw(seeds[0], (N_SPACE * 8, HALF, HALF, HALF, CIN), 1.0, 6.0, ((0, 512),)),
        "kernel_one": bell_draw(seeds[1], (3, 3, 3, CIN, F1), (27 * CIN) ** -0.5, 0.109375),
        "bias_one": bell_draw(seeds[2], (F1,), 0.5, 3.0, (), jnp.float32),
        "kernel_two": bell_draw(seeds[3], (3, 3, 3, F1, F2), (27 * F1) ** -0.5, 0.078125, ((4, 8),)),
        "bias_two": bell_draw(seeds[4], (F2,), 0.5, 3.0, ((0, 8),), jnp.float32),
    }


def convolve(volume, kernel, bias):
    result = lax.conv_general_dilated(volume[None].astype(jnp.float32), kernel.astype(jnp.float32), (1, 1, 1), "SAME", dimension_numbers=("NDHWC", "DHWIO", "NDHWC"), precision=lax.Precision.HIGHEST)[0]
    return jnp.maximum(result + bias, 0.0).astype(jnp.bfloat16)


def reference(blocks, kernel_one, bias_one, kernel_two, bias_two):
    volume = blocks.reshape(GX, GY, GZ, 2, 2, 2, HALF, HALF, HALF, CIN)
    volume = volume.transpose(0, 3, 6, 1, 4, 7, 2, 5, 8, 9).reshape(NX, NY, NZ, CIN)
    hidden = convolve(volume, kernel_one, bias_one)
    output = convolve(hidden, kernel_two, bias_two)
    tiles = output.reshape(GX, TILE, GY, TILE, GZ, TILE, F2).transpose(0, 2, 4, 1, 3, 5, 6)
    return tiles.reshape(GX * GY * GZ, TILE, TILE, TILE, F2)
```

```python
import jax
import jax.numpy as jnp
import numpy as np
from jax import lax
from jax.experimental import pallas as pl
from jax.experimental.pallas import tpu as pltpu
from jax.sharding import PartitionSpec as P

MESH = pl.DeviceIdType.MESH
G = 4
PIECES = (
    ((1, 0, 0), 64, 32),
    ((0, 1, 0), 96, 32),
    ((0, 0, 1), 128, 32),
    ((1, 1, 0), 160, 16),
    ((1, 0, 1), 176, 16),
    ((0, 1, 1), 192, 16),
    ((1, 1, 1), 208, 16),
)
OWN = 64
SLOT = 224
RIM = SLOT - OWN


def unpack_matrix():
    def place(n):
        if n < 2:
            return 1, True, n
        if n < 6:
            return 0, False, n - 2
        if n < 10:
            return 1, False, n - 6
        return 0, True, n - 10

    out = np.zeros((4, 3, 12, 16, 256), np.float32)
    for u in range(4):
        for shift in range(3):
            for y in range(12):
                for z in range(10):
                    b, rim_y, v = place(y)
                    c, rim_z, w = place(z + shift)
                    at = (2 * b + c) * 64
                    if rim_y and rim_z:
                        at += 48 + u * 4 + v * 2 + w
                    elif rim_z:
                        at += 32 + (u % 2) * 8 + v * 2 + w
                    elif rim_y:
                        at += 16 + (u % 2) * 8 + v * 4 + w
                    else:
                        at += v * 4 + w
                    out[u, shift, y, z, at] = 1
    return out.reshape(4, 576, 256).astype(jnp.bfloat16)


def kernel(
    x_ref, k1_hbm, b1_ref, k2_hbm, b2_ref, p_hbm, out_ref,
    land, pack, k1, k2, pick, wide, hidden, mask,
    load_sem, a_send, a_recv, b_send, b_recv, c_send, c_recv,
):
    space, chan = lax.axis_index("space"), lax.axis_index("chan")
    i, j, k = space // (G * G), space // G % G, space % G
    oct_a, oct_b, oct_c = chan // 4, chan // 2 % 2, chan % 2

    loads = [
        pltpu.make_async_copy(src, dst, load_sem.at[n])
        for n, (src, dst) in enumerate(((p_hbm, pick), (k1_hbm, k1), (k2_hbm, k2)))
    ]
    for load in loads:
        load.start()

    def tile(way, sign):
        ti = (i + sign * way[0] * (2 * oct_a - 1) + G) % G
        tj = (j + sign * way[1] * (2 * oct_b - 1) + G) % G
        tk = (k + sign * way[2] * (2 * oct_c - 1) + G) % G
        return (ti * G + tj) * G + tk

    barrier = pltpu.get_barrier_semaphore()
    for way, _, _ in PIECES:
        pl.semaphore_signal(barrier, inc=1, device_id=(tile(way, -1), chan), device_id_type=MESH)
    for d in range(1, 8):
        pl.semaphore_signal(barrier, inc=1, device_id=(space, (chan + d) % 8), device_id_type=MESH)

    x = x_ref[...]
    r = lax.broadcasted_iota(jnp.int32, (RIM, OWN), 0)
    col = lax.broadcasted_iota(jnp.int32, (RIM, OWN), 1)
    xs, ys, zs = 32 * oct_a, 8 * oct_b, 2 * oct_c
    src = jnp.full((RIM, OWN), -1, jnp.int32)
    ok_x = (i + 2 * oct_a - 1 >= 0) & (i + 2 * oct_a - 1 < G)
    ok_y = (j + 2 * oct_b - 1 >= 0) & (j + 2 * oct_b - 1 < G)
    ok_z = (k + 2 * oct_c - 1 >= 0) & (k + 2 * oct_c - 1 < G)
    for way, start, rows in PIECES:
        q = r - (start - OWN)
        at = jnp.zeros_like(r)
        if way[2]:
            at = at + zs + (q & 1)
            q = q >> 1
        else:
            at = at + (q & 3)
            q = q >> 2
        if way[1]:
            at = at + ys + 4 * (q & 1)
            q = q >> 1
        else:
            at = at + 4 * (q & 3)
            q = q >> 2
        at = at + 16 * q + (xs if way[0] else 0)
        if way == (1, 1, 1):
            rows = 8
        ok = jnp.int32(1)
        for crosses, fine in zip(way, (ok_x, ok_y, ok_z)):
            if crosses:
                ok = ok * fine.astype(jnp.int32)
        at = jnp.where(ok == 1, at, -1)
        inside = (r >= start - OWN) & (r < start - OWN + rows)
        src = jnp.where(inside, at, src)
    select = jnp.where(src == col, 1.0, 0.0).astype(jnp.bfloat16)
    pack[...] = jnp.dot(select, x, preferred_element_type=jnp.float32).astype(jnp.bfloat16)
    land[chan, 0:OWN] = x

    pl.semaphore_wait(barrier, 14)

    rims = []
    for n, (way, start, rows) in enumerate(PIECES):
        rims.append(
            pltpu.make_async_remote_copy(
                src_ref=pack.at[pl.ds(start - OWN, rows)],
                dst_ref=land.at[chan, pl.ds(start, rows)],
                send_sem=a_send.at[n],
                recv_sem=a_recv.at[n],
                device_id=(tile(way, 1), chan),
                device_id_type=MESH,
            )
        )
        rims[-1].start()
    owns, relays = [], []
    for d in range(1, 8):
        to = (space, (chan + d) % 8)
        owns.append(
            pltpu.make_async_remote_copy(
                src_ref=x_ref,
                dst_ref=land.at[chan, pl.ds(0, OWN)],
                send_sem=b_send.at[d - 1],
                recv_sem=b_recv.at[d - 1],
                device_id=to,
                device_id_type=MESH,
            )
        )
        owns[-1].start()
        relays.append(
            pltpu.make_async_remote_copy(
                src_ref=land.at[chan, pl.ds(OWN, RIM)],
                dst_ref=land.at[chan, pl.ds(OWN, RIM)],
                send_sem=c_send.at[d - 1],
                recv_sem=c_recv.at[d - 1],
                device_id=to,
                device_id_type=MESH,
            )
        )
    row = lax.broadcasted_iota(jnp.int32, (160, 256), 0)
    hy, hz = row >> 4, row & 15
    outside = ((j == 0) & (hy == 0)) | ((j == G - 1) & (hy == 9))
    outside = outside | ((k == 0) & (hz == 0)) | ((k == G - 1) & (hz == 9))
    mask[...] = jnp.where(outside, 0.0, 1.0)

    for copy in rims:
        copy.wait_recv()
    for copy in relays:
        copy.start()
    for copy in owns:
        copy.wait_recv()
    for load in loads:
        load.wait()
    for copy in relays:
        copy.wait_recv()

    def unpack(u, chunks, x_of):
        sides = []
        for a in range(2):
            parts = []
            for s in range(4):
                for chunk in chunks:
                    parts.append(land[a * 4 + s, pl.ds(pl.multiple_of(chunk, 16), 16)])
            sides.append(jnp.concatenate(parts, axis=0))
        voxels = jnp.concatenate(sides, axis=1)
        got = jnp.dot(pick[u], voxels, preferred_element_type=jnp.float32).astype(jnp.bfloat16)
        for a in range(2):
            for shift in range(3):
                piece = got[shift * 192 : (shift + 1) * 192, a * 128 : (a + 1) * 128]
                wide[x_of[a], :, :, shift * 128 : (shift + 1) * 128] = piece.reshape(12, 16, 128)

    def own_plane(u, _):
        unpack(u, (16 * u, 96 + 16 * (u // 2), 128 + 16 * (u // 2), 192), (2 + u, 6 + u))
        return 0

    def rim_plane(h, _):
        unpack(h, (64 + 16 * h, 160, 176, 208), (10 + h, h))
        return 0

    lax.fori_loop(0, 4, own_plane, 0)
    lax.fori_loop(0, 2, rim_plane, 0)

    bias_one = b1_ref[...]

    def first(n, _):
        at = 2 * n
        taps = [
            wide[pl.ds(at + a, 2), b : b + 10].reshape(320, 384) for a in range(3) for b in range(3)
        ]
        total = jnp.dot(jnp.concatenate(taps, axis=1), k1[...], preferred_element_type=jnp.float32)
        total = jnp.maximum(total + bias_one, 0.0)
        for p in range(2):
            inside = ((at + p > 0) | (i > 0)) & ((at + p < 9) | (i < G - 1))
            keep = mask[...] * jnp.where(inside, 1.0, 0.0)
            plane = total[p * 160 : (p + 1) * 160] * keep
            hidden[at + p] = plane.astype(jnp.bfloat16).reshape(10, 16, 256)
        return 0

    lax.fori_loop(0, 5, first, 0)

    bias_two = b2_ref[...]

    def second(n, _):
        at = 4 * n
        total = jnp.zeros((512, 96), jnp.float32)
        for a in range(3):
            for b in range(3):
                voxels = hidden[pl.ds(at + a, 4), b : b + 8].reshape(512, 256)
                total = total + lax.dot_general(
                    voxels, k2[3 * a + b], (((1,), (1,)), ((), ())), preferred_element_type=jnp.float32
                )
        total = total.reshape(32, 16, 96)
        result = total[:, 0:8, 0:32] + total[:, 1:9, 32:64] + total[:, 2:10, 64:96] + bias_two
        result = jnp.maximum(result, 0.0).astype(jnp.bfloat16)
        out_ref[pl.ds(pl.multiple_of(n * 32, 32), 32)] = result
        return 0

    lax.fori_loop(0, 2, second, 0)

    for copy in rims + owns + relays:
        copy.wait_send()


def on_device(blocks, kernel_one, bias_one, kernel_two, bias_two):
    cin, f1 = kernel_one.shape[3:]
    f2 = kernel_two.shape[4]
    vmem, anywhere = pl.BlockSpec(memory_space=pltpu.VMEM), pl.BlockSpec(memory_space=pl.ANY)
    dma = pltpu.SemaphoreType.DMA
    out = pl.pallas_call(
        kernel,
        out_shape=jax.ShapeDtypeStruct((64, 8, f2), jnp.bfloat16),
        in_specs=[vmem, anywhere, vmem, anywhere, vmem, anywhere],
        out_specs=vmem,
        scratch_shapes=[
            pltpu.VMEM((8, SLOT, cin), jnp.bfloat16),
            pltpu.VMEM((RIM, cin), jnp.bfloat16),
            pltpu.VMEM((27 * cin, f1), jnp.bfloat16),
            pltpu.VMEM((9, 3 * f2, f1), jnp.bfloat16),
            pltpu.VMEM((4, 576, 256), jnp.bfloat16),
            pltpu.VMEM((12, 12, 16, 3 * cin), jnp.bfloat16),
            pltpu.VMEM((10, 10, 16, f1), jnp.bfloat16),
            pltpu.VMEM((160, f1), jnp.float32),
            dma((3,)), dma((7,)), dma((7,)), dma((7,)), dma((7,)), dma((7,)), dma((7,)),
        ],
        compiler_params=pltpu.CompilerParams(
            collective_id=0, has_side_effects=True, vmem_limit_bytes=48 * 1024 * 1024
        ),
        cost_estimate=pl.CostEstimate(flops=2_000_000_000, bytes_accessed=4_000_000, transcendentals=0),
    )(
        blocks.reshape(64, cin),
        kernel_one.reshape(27 * cin, f1),
        bias_one.reshape(1, f1),
        kernel_two.transpose(0, 1, 2, 4, 3).reshape(9, 3 * f2, f1),
        bias_two.reshape(1, f2),
        jnp.asarray(unpack_matrix()),
    )
    return out.reshape(1, 8, 8, 8, f2)


def solution(mesh):
    placed = (
        P(("space", "chan"), None, None, None, None),
        P(),
        P(),
        P(None, None, None, None, "chan"),
        P("chan"),
    )
    return jax.shard_map(
        on_device,
        mesh=mesh,
        in_specs=placed,
        out_specs=P("space", None, None, None, "chan"),
        check_vma=False,
    )
```

```python
import jax
import jax.numpy as jnp
import numpy as np
from jax import lax
from jax.experimental import pallas as pl
from jax.experimental.pallas import tpu as pltpu
from jax.sharding import PartitionSpec as P

MESH = pl.DeviceIdType.MESH
G = 4
PIECES = (
    ((0, 0, 1), 64, 32),
    ((1, 0, 0), 96, 32),
    ((1, 0, 1), 128, 16),
    ((0, 1, 0), 144, 32),
    ((0, 1, 1), 176, 16),
    ((1, 1, 0), 192, 16),
    ((1, 1, 1), 208, 16),
)
NEAR = 3
OWN = 64
SLOT = 224
RIM = SLOT - OWN
HALF = RIM // 2


def unpack_matrices():
    def place(n):
        if n < 2:
            return 1, n
        return (1, n - 6) if n >= 6 and n < 10 else (0, (n - 2) % 8)

    inner = np.zeros((2, 3, 8, 16, 128), np.float32)
    outer = np.zeros((4, 3, 4, 16, 128), np.float32)
    for shift in range(3):
        for z in range(10):
            c, w = place(z + shift)
            rim = z + shift < 2 or z + shift >= 10
            for u in range(2):
                for y in range(8):
                    at = (2 * (y // 4) + c) * 32
                    v = y % 4
                    inner[u, shift, y, z, at + (16 + u * 8 + v * 2 + w if rim else v * 4 + w)] = 1
            for u in range(4):
                for y in range(4):
                    at = (2 * (1 - y // 2) + c) * 32
                    v = y % 2
                    outer[u, shift, y, z, at + (16 + u * 4 + v * 2 + w if rim else (u % 2) * 8 + v * 4 + w)] = 1
    return inner.reshape(2, 384, 128).astype(jnp.bfloat16), outer.reshape(4, 192, 128).astype(jnp.bfloat16)


def kernel(
    x_hbm, k1_hbm, b1_hbm, k2_hbm, b2_hbm, p_hbm, q_hbm, out_ref,
    x_ref, b1_ref, b2_ref, land, pack, k1, k2, k2_t, pick, pick_rim, wide, hidden, mask,
    load_sem, a_send, a_recv, b_send, b_recv, c_send, c_recv, d_send, d_recv,
):
    space, chan = lax.axis_index("space"), lax.axis_index("chan")
    i, j, k = space // (G * G), space // G % G, space % G
    oct_a, oct_b, oct_c = chan // 4, chan // 2 % 2, chan % 2

    def tile(way, sign):
        ti = (i + sign * way[0] * (2 * oct_a - 1) + G) % G
        tj = (j + sign * way[1] * (2 * oct_b - 1) + G) % G
        tk = (k + sign * way[2] * (2 * oct_c - 1) + G) % G
        return (ti * G + tj) * G + tk

    barrier = pltpu.get_barrier_semaphore()
    for way, _, _ in PIECES[::-1]:
        pl.semaphore_signal(barrier, inc=1, device_id=(tile(way, -1), chan), device_id_type=MESH)
    for d in range(1, 8):
        pl.semaphore_signal(barrier, inc=1, device_id=(space, (chan + d) % 8), device_id_type=MESH)

    pairs = (x_hbm, x_ref), (p_hbm, pick), (q_hbm, pick_rim), (k1_hbm, k1), (k2_hbm, k2), (b1_hbm, b1_ref), (b2_hbm, b2_ref)
    loads = [
        pltpu.make_async_copy(src, dst, load_sem.at[n]) for n, (src, dst) in enumerate(pairs)
    ]
    for load in loads:
        load.start()

    r = lax.broadcasted_iota(jnp.int32, (RIM, OWN), 0)
    col = lax.broadcasted_iota(jnp.int32, (RIM, OWN), 1)
    xs, ys, zs = 32 * oct_a, 8 * oct_b, 2 * oct_c
    src = jnp.full((RIM, OWN), -1, jnp.int32)
    ok_x = (i + 2 * oct_a - 1 >= 0) & (i + 2 * oct_a - 1 < G)
    ok_y = (j + 2 * oct_b - 1 >= 0) & (j + 2 * oct_b - 1 < G)
    ok_z = (k + 2 * oct_c - 1 >= 0) & (k + 2 * oct_c - 1 < G)
    for way, start, rows in PIECES:
        q = r - (start - OWN)
        at = jnp.zeros_like(r)
        if way[2]:
            at = at + zs + (q & 1)
            q = q >> 1
        else:
            at = at + (q & 3)
            q = q >> 2
        if way[1]:
            at = at + ys + 4 * (q & 1)
            q = q >> 1
        else:
            at = at + 4 * (q & 3)
            q = q >> 2
        at = at + 16 * q + (xs if way[0] else 0)
        if way == (1, 1, 1):
            rows = 8
        ok = jnp.int32(1)
        for crosses, fine in zip(way, (ok_x, ok_y, ok_z)):
            if crosses:
                ok = ok * fine.astype(jnp.int32)
        at = jnp.where(ok == 1, at, -1)
        inside = (r >= start - OWN) & (r < start - OWN + rows)
        src = jnp.where(inside, at, src)
    loads[0].wait()
    x = x_ref[...]
    select = jnp.where(src == col, 1.0, 0.0).astype(jnp.bfloat16)
    pack[...] = jnp.dot(select, x, preferred_element_type=jnp.float32).astype(jnp.bfloat16)
    land[chan, 0:OWN] = x

    pl.semaphore_wait(barrier, 14)

    rims = []
    for n, (way, start, rows) in enumerate(PIECES):
        rims.append(
            pltpu.make_async_remote_copy(
                src_ref=pack.at[pl.ds(start - OWN, rows)],
                dst_ref=land.at[chan, pl.ds(start, rows)],
                send_sem=a_send.at[n],
                recv_sem=a_recv.at[n],
                device_id=(tile(way, 1), chan),
                device_id_type=MESH,
            )
        )
    for copy in rims[::-1]:
        copy.start()

    def to_tile(src_of, start, rows, send_sem, recv_sem):
        return [
            pltpu.make_async_remote_copy(
                src_ref=src_of,
                dst_ref=land.at[chan, pl.ds(start, rows)],
                send_sem=send_sem.at[d - 1],
                recv_sem=recv_sem.at[d - 1],
                device_id=(space, (chan + d) % 8),
                device_id_type=MESH,
            )
            for d in range(1, 8)
        ]

    owns = to_tile(x_ref, 0, OWN, b_send, b_recv)
    near = to_tile(land.at[chan, pl.ds(OWN, HALF)], OWN, HALF, c_send, c_recv)
    far = to_tile(land.at[chan, pl.ds(OWN + HALF, HALF)], OWN + HALF, HALF, d_send, d_recv)
    for copy in owns:
        copy.start()

    row = lax.broadcasted_iota(jnp.int32, (160, 256), 0)
    hy, hz = row >> 4, row & 15
    outside = ((j == 0) & (hy == 0)) | ((j == G - 1) & (hy == 9))
    outside = outside | ((k == 0) & (hz == 0)) | ((k == G - 1) & (hz == 9))
    mask[...] = jnp.where(outside, 0.0, 1.0).reshape(10, 16, 256)
    for load in loads[1:]:
        load.wait()
    for n in range(9):
        k2_t[n * 256 : (n + 1) * 256, :] = k2[n].T

    for copy in rims[:NEAR]:
        copy.wait_recv()
    for copy in near:
        copy.start()
    for copy in rims[NEAR:]:
        copy.wait_recv()
    for copy in far:
        copy.start()
    for copy in owns:
        copy.wait_recv()
    for copy in near:
        copy.wait_recv()

    def unpack(matrix, chunks, x_of, y_of):
        sides = []
        for a in range(2):
            parts = []
            for s in range(4):
                for chunk in chunks:
                    parts.append(land[a * 4 + s, chunk : chunk + 16])
            sides.append(jnp.concatenate(parts, axis=0))
        voxels = jnp.concatenate(sides, axis=1)
        got = jnp.dot(matrix, voxels, preferred_element_type=jnp.float32).astype(jnp.bfloat16)
        rows = got.shape[0] // 3
        for a in range(2):
            for shift in range(3):
                piece = got[shift * rows : (shift + 1) * rows, a * 128 : (a + 1) * 128]
                piece = piece.reshape(rows // 16, 16, 128)
                at = 0
                for y, count in y_of:
                    wide[x_of[a], y : y + count, :, shift * 128 : (shift + 1) * 128] = piece[at : at + count]
                    at += count

    bias_one, bias_two = b1_ref[...], b2_ref[...]

    def stack(ref, at, planes, shift, y_of):
        parts = [ref[at : at + planes, y + shift : y + shift + count] for y, count in y_of]
        whole = jnp.concatenate(parts, axis=1) if len(parts) > 1 else parts[0]
        return whole.reshape(-1, whole.shape[3])

    def first(at, planes, y_of):
        taps = [stack(wide, at + a, planes, b, y_of) for a in range(3) for b in range(3)]
        total = jnp.dot(jnp.concatenate(taps, axis=1), k1[...], preferred_element_type=jnp.float32)
        total = jnp.maximum(total + bias_one, 0.0).reshape(planes, -1, 16, 256)
        for p in range(planes):
            inside = ((at + p > 0) | (i > 0)) & ((at + p < 9) | (i < G - 1))
            keep = jnp.where(inside, 1.0, 0.0)
            row = 0
            for y, count in y_of:
                plane = total[p, row : row + count] * (mask[y : y + count] * keep)
                hidden[at + p, y : y + count] = plane.astype(jnp.bfloat16)
                row += count

    def second(at, planes, y_of):
        taps = [stack(hidden, at + a, planes, b, y_of) for a in range(3) for b in range(3)]
        total = jnp.dot(jnp.concatenate(taps, axis=1), k2_t[...], preferred_element_type=jnp.float32)
        total = total.reshape(-1, 16, 96)
        result = total[:, 0:8, 0:32] + total[:, 1:9, 32:64] + total[:, 2:10, 64:96] + bias_two
        result = jnp.maximum(result, 0.0).astype(jnp.bfloat16).reshape(planes, -1, 8, 32)
        row = 0
        for y, count in y_of:
            out_ref[at : at + planes, y : y + count] = result[:, row : row + count]
            row += count

    def inner(p):
        for n in range(2):
            u = p + 2 * n
            unpack(pick[p], (16 * u, 64 + 16 * n), (2 + u, 6 + u), ((2, 8),))
        unpack(pick[p], (96 + 16 * p, 128), (10 + p, p), ((2, 8),))

    def outer(p):
        for n in range(2):
            u = p + 2 * n
            unpack(pick_rim[u], (144 + 16 * n, 176), (2 + u, 6 + u), ((0, 2), (10, 2)))
        unpack(pick_rim[p], (192, 208), (10 + p, p), ((0, 2), (10, 2)))

    inner(0)
    inner(1)
    first(0, 5, ((2, 6),))
    first(5, 5, ((2, 6),))
    second(0, 4, ((2, 4),))
    second(4, 4, ((2, 4),))

    for copy in far:
        copy.wait_recv()
    outer(0)
    outer(1)
    first(0, 5, ((0, 2), (8, 2)))
    first(5, 5, ((0, 2), (8, 2)))
    second(0, 4, ((0, 2), (6, 2)))
    second(4, 4, ((0, 2), (6, 2)))

    for copy in rims + owns + near + far:
        copy.wait_send()


def on_device(blocks, kernel_one, bias_one, kernel_two, bias_two):
    cin, f1 = kernel_one.shape[3:]
    f2 = kernel_two.shape[4]
    vmem, hbm = pl.BlockSpec(memory_space=pltpu.VMEM), pl.BlockSpec(memory_space=pltpu.HBM)
    dma = pltpu.SemaphoreType.DMA
    out = pl.pallas_call(
        kernel,
        out_shape=jax.ShapeDtypeStruct((8, 8, 8, f2), jnp.bfloat16),
        in_specs=[hbm] * 7,
        out_specs=vmem,
        scratch_shapes=[
            pltpu.VMEM((OWN, cin), jnp.bfloat16),
            pltpu.VMEM((1, f1), jnp.float32),
            pltpu.VMEM((1, f2), jnp.float32),
            pltpu.VMEM((8, SLOT, cin), jnp.bfloat16),
            pltpu.VMEM((RIM, cin), jnp.bfloat16),
            pltpu.VMEM((27 * cin, f1), jnp.bfloat16),
            pltpu.VMEM((9, 3 * f2, f1), jnp.bfloat16),
            pltpu.VMEM((9 * f1, 3 * f2), jnp.bfloat16),
            pltpu.VMEM((2, 384, 128), jnp.bfloat16),
            pltpu.VMEM((4, 192, 128), jnp.bfloat16),
            pltpu.VMEM((12, 12, 16, 3 * cin), jnp.bfloat16),
            pltpu.VMEM((10, 10, 16, f1), jnp.bfloat16),
            pltpu.VMEM((10, 16, f1), jnp.float32),
            dma((7,)), dma((7,)), dma((7,)), dma((7,)), dma((7,)), dma((7,)), dma((7,)), dma((7,)), dma((7,)),
        ],
        compiler_params=pltpu.CompilerParams(
            collective_id=0, has_side_effects=True, vmem_limit_bytes=64 * 1024 * 1024
        ),
        cost_estimate=pl.CostEstimate(flops=2_000_000_000, bytes_accessed=4_000_000, transcendentals=0),
    )(
        blocks.reshape(64, cin),
        kernel_one.reshape(27 * cin, f1),
        bias_one.reshape(1, f1),
        kernel_two.transpose(0, 1, 2, 4, 3).reshape(9, 3 * f2, f1),
        bias_two.reshape(1, f2),
        *(jnp.asarray(matrix) for matrix in unpack_matrices()),
    )
    return out.reshape(1, 8, 8, 8, f2)


def solution(mesh):
    placed = (
        P(("space", "chan"), None, None, None, None),
        P(),
        P(),
        P(None, None, None, None, "chan"),
        P("chan"),
    )
    return jax.shard_map(
        on_device,
        mesh=mesh,
        in_specs=placed,
        out_specs=P("space", None, None, None, "chan"),
        check_vma=False,
    )
```

```python
import jax
import jax.numpy as jnp
import numpy as np
from jax import lax
from jax.experimental import pallas as pl
from jax.experimental.pallas import tpu as pltpu
from jax.sharding import PartitionSpec as P

MESH = pl.DeviceIdType.MESH
G = 4
PIECES = (
    ((0, 0, 1), 64, 32),
    ((1, 0, 0), 96, 32),
    ((1, 0, 1), 128, 16),
    ((0, 1, 0), 144, 32),
    ((0, 1, 1), 176, 16),
    ((1, 1, 0), 192, 16),
    ((1, 1, 1), 208, 16),
)
NEAR = 3
OWN = 64
SLOT = 224
RIM = SLOT - OWN
HALF = RIM // 2


def unpack_matrices():
    def place(n):
        if n < 2:
            return 1, n
        return (1, n - 6) if n >= 6 and n < 10 else (0, (n - 2) % 8)

    inner = np.zeros((2, 3, 8, 16, 128), np.float32)
    outer = np.zeros((4, 3, 4, 16, 128), np.float32)
    for shift in range(3):
        for z in range(10):
            c, w = place(z + shift)
            rim = z + shift < 2 or z + shift >= 10
            for u in range(2):
                for y in range(8):
                    at = (2 * (y // 4) + c) * 32
                    v = y % 4
                    inner[u, shift, y, z, at + (16 + u * 8 + v * 2 + w if rim else v * 4 + w)] = 1
            for u in range(4):
                for y in range(4):
                    at = (2 * (1 - y // 2) + c) * 32
                    v = y % 2
                    outer[u, shift, y, z, at + (16 + u * 4 + v * 2 + w if rim else (u % 2) * 8 + v * 4 + w)] = 1
    return inner.reshape(2, 384, 128).astype(jnp.bfloat16), outer.reshape(4, 192, 128).astype(jnp.bfloat16)


def kernel(
    x_hbm, k1_hbm, b1_hbm, k2_hbm, b2_hbm, p_hbm, q_hbm, out_ref,
    x_ref, b1_ref, b2_ref, land, pack, k1, k2, k2_t, pick, pick_rim, wide, hidden, mask,
    load_sem, a_send, a_recv, b_send, b_recv, c_send, c_recv, d_send, d_recv,
):
    space, chan = lax.axis_index("space"), lax.axis_index("chan")
    i, j, k = space // (G * G), space // G % G, space % G
    oct_a, oct_b, oct_c = chan // 4, chan // 2 % 2, chan % 2

    def tile(way, sign):
        ti = (i + sign * way[0] * (2 * oct_a - 1) + G) % G
        tj = (j + sign * way[1] * (2 * oct_b - 1) + G) % G
        tk = (k + sign * way[2] * (2 * oct_c - 1) + G) % G
        return (ti * G + tj) * G + tk

    def exists(way, sign):
        found = True
        for crosses, at, bit in zip(way, (i, j, k), (oct_a, oct_b, oct_c)):
            if crosses:
                to = at + sign * (2 * bit - 1)
                found = (to >= 0) & (to < G) & found
        return found

    gives = [exists(way, 1) for way, _, _ in PIECES]
    takes = [exists(way, -1) for way, _, _ in PIECES]

    barrier = pltpu.get_barrier_semaphore()
    for n in reversed(range(7)):

        @pl.when(takes[n])
        def _():
            to = (tile(PIECES[n][0], -1), chan)
            pl.semaphore_signal(barrier, inc=1, device_id=to, device_id_type=MESH)

    for d in range(1, 8):
        pl.semaphore_signal(barrier, inc=1, device_id=(space, (chan + d) % 8), device_id_type=MESH)

    pairs = (x_hbm, x_ref), (p_hbm, pick), (q_hbm, pick_rim), (k1_hbm, k1), (k2_hbm, k2), (b1_hbm, b1_ref), (b2_hbm, b2_ref)
    loads = [
        pltpu.make_async_copy(src, dst, load_sem.at[n]) for n, (src, dst) in enumerate(pairs)
    ]
    for load in loads:
        load.start()

    r = lax.broadcasted_iota(jnp.int32, (RIM, OWN), 0)
    col = lax.broadcasted_iota(jnp.int32, (RIM, OWN), 1)
    xs, ys, zs = 32 * oct_a, 8 * oct_b, 2 * oct_c
    src = jnp.full((RIM, OWN), -1, jnp.int32)
    for way, start, rows in PIECES:
        q = r - (start - OWN)
        at = jnp.zeros_like(r)
        if way[2]:
            at = at + zs + (q & 1)
            q = q >> 1
        else:
            at = at + (q & 3)
            q = q >> 2
        if way[1]:
            at = at + ys + 4 * (q & 1)
            q = q >> 1
        else:
            at = at + 4 * (q & 3)
            q = q >> 2
        at = at + 16 * q + (xs if way[0] else 0)
        if way == (1, 1, 1):
            rows = 8
        inside = (r >= start - OWN) & (r < start - OWN + rows)
        src = jnp.where(inside, at, src)
    loads[0].wait()
    x = x_ref[...]
    select = jnp.where(src == col, 1.0, 0.0).astype(jnp.bfloat16)
    pack[...] = jnp.dot(select, x, preferred_element_type=jnp.float32).astype(jnp.bfloat16)
    land[chan, 0:OWN] = x

    for n, (_, start, rows) in enumerate(PIECES):

        @pl.when(~takes[n])
        def _():
            land[chan, start : start + rows] = jnp.zeros((rows, 128), jnp.bfloat16)

    pl.semaphore_wait(barrier, 7 + sum(give.astype(jnp.int32) for give in gives))

    rims = []
    for n, (way, start, rows) in enumerate(PIECES):
        rims.append(
            pltpu.make_async_remote_copy(
                src_ref=pack.at[pl.ds(start - OWN, rows)],
                dst_ref=land.at[chan, pl.ds(start, rows)],
                send_sem=a_send.at[n],
                recv_sem=a_recv.at[n],
                device_id=(tile(way, 1), chan),
                device_id_type=MESH,
            )
        )
    for n in reversed(range(7)):
        pl.when(gives[n])(rims[n].start)

    def to_tile(src_of, start, rows, send_sem, recv_sem):
        return [
            pltpu.make_async_remote_copy(
                src_ref=src_of,
                dst_ref=land.at[chan, pl.ds(start, rows)],
                send_sem=send_sem.at[d - 1],
                recv_sem=recv_sem.at[d - 1],
                device_id=(space, (chan + d) % 8),
                device_id_type=MESH,
            )
            for d in range(1, 8)
        ]

    owns = to_tile(x_ref, 0, OWN, b_send, b_recv)
    near = to_tile(land.at[chan, pl.ds(OWN, HALF)], OWN, HALF, c_send, c_recv)
    far = to_tile(land.at[chan, pl.ds(OWN + HALF, HALF)], OWN + HALF, HALF, d_send, d_recv)
    for copy in owns:
        copy.start()

    row = lax.broadcasted_iota(jnp.int32, (160, 256), 0)
    hy, hz = row >> 4, row & 15
    outside = ((j == 0) & (hy == 0)) | ((j == G - 1) & (hy == 9))
    outside = outside | ((k == 0) & (hz == 0)) | ((k == G - 1) & (hz == 9))
    mask[...] = jnp.where(outside, 0.0, 1.0).reshape(10, 16, 256)
    for load in loads[1:]:
        load.wait()
    for n in range(9):
        k2_t[n * 256 : (n + 1) * 256, :] = k2[n].T

    for n in range(NEAR):
        pl.when(takes[n])(rims[n].wait_recv)
    for copy in near:
        copy.start()
    for n in range(NEAR, 7):
        pl.when(takes[n])(rims[n].wait_recv)
    for copy in far:
        copy.start()
    for copy in owns:
        copy.wait_recv()
    for copy in near:
        copy.wait_recv()

    def unpack(matrix, chunks, x_of, y_of):
        sides = []
        for a in range(2):
            parts = []
            for s in range(4):
                for chunk in chunks:
                    parts.append(land[a * 4 + s, chunk : chunk + 16])
            sides.append(jnp.concatenate(parts, axis=0))
        voxels = jnp.concatenate(sides, axis=1)
        got = jnp.dot(matrix, voxels, preferred_element_type=jnp.float32).astype(jnp.bfloat16)
        rows = got.shape[0] // 3
        for a in range(2):
            for shift in range(3):
                piece = got[shift * rows : (shift + 1) * rows, a * 128 : (a + 1) * 128]
                piece = piece.reshape(rows // 16, 16, 128)
                at = 0
                for y, count in y_of:
                    wide[x_of[a], y : y + count, :, shift * 128 : (shift + 1) * 128] = piece[at : at + count]
                    at += count

    bias_one, bias_two = b1_ref[...], b2_ref[...]

    def stack(ref, at, planes, shift, y_of):
        parts = [ref[at : at + planes, y + shift : y + shift + count] for y, count in y_of]
        whole = jnp.concatenate(parts, axis=1) if len(parts) > 1 else parts[0]
        return whole.reshape(-1, whole.shape[3])

    def first(at, planes, y_of):
        taps = [stack(wide, at + a, planes, b, y_of) for a in range(3) for b in range(3)]
        total = jnp.dot(jnp.concatenate(taps, axis=1), k1[...], preferred_element_type=jnp.float32)
        total = jnp.maximum(total + bias_one, 0.0).reshape(planes, -1, 16, 256)
        for p in range(planes):
            inside = ((at + p > 0) | (i > 0)) & ((at + p < 9) | (i < G - 1))
            keep = jnp.where(inside, 1.0, 0.0)
            row = 0
            for y, count in y_of:
                plane = total[p, row : row + count] * (mask[y : y + count] * keep)
                hidden[at + p, y : y + count] = plane.astype(jnp.bfloat16)
                row += count

    def second(at, planes, y_of):
        taps = [stack(hidden, at + a, planes, b, y_of) for a in range(3) for b in range(3)]
        total = jnp.dot(jnp.concatenate(taps, axis=1), k2_t[...], preferred_element_type=jnp.float32)
        total = total.reshape(-1, 16, 96)
        result = total[:, 0:8, 0:32] + total[:, 1:9, 32:64] + total[:, 2:10, 64:96] + bias_two
        result = jnp.maximum(result, 0.0).astype(jnp.bfloat16).reshape(planes, -1, 8, 32)
        row = 0
        for y, count in y_of:
            out_ref[at : at + planes, y : y + count] = result[:, row : row + count]
            row += count

    def inner(p):
        for n in range(2):
            u = p + 2 * n
            unpack(pick[p], (16 * u, 64 + 16 * n), (2 + u, 6 + u), ((2, 8),))
        unpack(pick[p], (96 + 16 * p, 128), (10 + p, p), ((2, 8),))

    def outer(p):
        for n in range(2):
            u = p + 2 * n
            unpack(pick_rim[u], (144 + 16 * n, 176), (2 + u, 6 + u), ((0, 2), (10, 2)))
        unpack(pick_rim[p], (192, 208), (10 + p, p), ((0, 2), (10, 2)))

    inner(0)
    inner(1)
    first(0, 5, ((2, 6),))
    first(5, 5, ((2, 6),))
    second(0, 4, ((2, 4),))
    second(4, 4, ((2, 4),))

    for copy in far:
        copy.wait_recv()
    outer(0)
    outer(1)
    first(0, 5, ((0, 2), (8, 2)))
    first(5, 5, ((0, 2), (8, 2)))
    second(0, 4, ((0, 2), (6, 2)))
    second(4, 4, ((0, 2), (6, 2)))

    for n in range(7):
        pl.when(gives[n])(rims[n].wait_send)
    for copy in owns + near + far:
        copy.wait_send()


def on_device(blocks, kernel_one, bias_one, kernel_two, bias_two):
    cin, f1 = kernel_one.shape[3:]
    f2 = kernel_two.shape[4]
    vmem, hbm = pl.BlockSpec(memory_space=pltpu.VMEM), pl.BlockSpec(memory_space=pltpu.HBM)
    dma = pltpu.SemaphoreType.DMA
    out = pl.pallas_call(
        kernel,
        out_shape=jax.ShapeDtypeStruct((8, 8, 8, f2), jnp.bfloat16),
        in_specs=[hbm] * 7,
        out_specs=vmem,
        scratch_shapes=[
            pltpu.VMEM((OWN, cin), jnp.bfloat16),
            pltpu.VMEM((1, f1), jnp.float32),
            pltpu.VMEM((1, f2), jnp.float32),
            pltpu.VMEM((8, SLOT, cin), jnp.bfloat16),
            pltpu.VMEM((RIM, cin), jnp.bfloat16),
            pltpu.VMEM((27 * cin, f1), jnp.bfloat16),
            pltpu.VMEM((9, 3 * f2, f1), jnp.bfloat16),
            pltpu.VMEM((9 * f1, 3 * f2), jnp.bfloat16),
            pltpu.VMEM((2, 384, 128), jnp.bfloat16),
            pltpu.VMEM((4, 192, 128), jnp.bfloat16),
            pltpu.VMEM((12, 12, 16, 3 * cin), jnp.bfloat16),
            pltpu.VMEM((10, 10, 16, f1), jnp.bfloat16),
            pltpu.VMEM((10, 16, f1), jnp.float32),
            dma((7,)), dma((7,)), dma((7,)), dma((7,)), dma((7,)), dma((7,)), dma((7,)), dma((7,)), dma((7,)),
        ],
        compiler_params=pltpu.CompilerParams(
            collective_id=0, has_side_effects=True, vmem_limit_bytes=64 * 1024 * 1024
        ),
        cost_estimate=pl.CostEstimate(flops=2_000_000_000, bytes_accessed=4_000_000, transcendentals=0),
    )(
        blocks.reshape(64, cin),
        kernel_one.reshape(27 * cin, f1),
        bias_one.reshape(1, f1),
        kernel_two.transpose(0, 1, 2, 4, 3).reshape(9, 3 * f2, f1),
        bias_two.reshape(1, f2),
        *(jnp.asarray(matrix) for matrix in unpack_matrices()),
    )
    return out.reshape(1, 8, 8, 8, f2)


def solution(mesh):
    placed = (
        P(("space", "chan"), None, None, None, None),
        P(),
        P(),
        P(None, None, None, None, "chan"),
        P("chan"),
    )
    return jax.shard_map(
        on_device,
        mesh=mesh,
        in_specs=placed,
        out_specs=P("space", None, None, None, "chan"),
        check_vma=False,
    )
```

```python
import jax
import jax.numpy as jnp
import numpy as np
from jax import lax
from jax.experimental import pallas as pl
from jax.experimental.pallas import tpu as pltpu
from jax.sharding import PartitionSpec as P

MESH = pl.DeviceIdType.MESH
G = 4
PIECES = (
    ((0, 0, 1), 64, 32),
    ((1, 0, 0), 96, 32),
    ((1, 0, 1), 128, 16),
    ((0, 1, 0), 144, 32),
    ((0, 1, 1), 176, 16),
    ((1, 1, 0), 192, 16),
    ((1, 1, 1), 208, 16),
)
NEAR = 3
OWN = 64
SLOT = 224
RIM = SLOT - OWN
HALF = RIM // 2


def unpack_matrices():
    def place(n):
        if n < 2:
            return 1, n
        return (1, n - 6) if n >= 6 and n < 10 else (0, (n - 2) % 8)

    inner = np.zeros((2, 3, 8, 16, 128), np.float32)
    outer = np.zeros((4, 3, 4, 16, 128), np.float32)
    for shift in range(3):
        for z in range(10):
            c, w = place(z + shift)
            rim = z + shift < 2 or z + shift >= 10
            for u in range(2):
                for y in range(8):
                    at = (2 * (y // 4) + c) * 32
                    v = y % 4
                    inner[u, shift, y, z, at + (16 + u * 8 + v * 2 + w if rim else v * 4 + w)] = 1
            for u in range(4):
                for y in range(4):
                    at = (2 * (1 - y // 2) + c) * 32
                    v = y % 2
                    outer[u, shift, y, z, at + (16 + u * 4 + v * 2 + w if rim else (u % 2) * 8 + v * 4 + w)] = 1
    return inner.reshape(2, 384, 128).astype(jnp.bfloat16), outer.reshape(4, 192, 128).astype(jnp.bfloat16)


def kernel(
    x_hbm, k1_hbm, b1_hbm, k2_hbm, b2_hbm, p_hbm, q_hbm, out_ref,
    x_ref, b1_ref, b2_ref, land, pack, k1, k2, k2_t, pick, pick_rim, wide, hidden, mask,
    load_sem, a_send, a_recv, b_send, b_recv, c_send, c_recv, d_send, d_recv, ready,
):
    space, chan = lax.axis_index("space"), lax.axis_index("chan")
    i, j, k = space // (G * G), space // G % G, space % G
    oct_a, oct_b, oct_c = chan // 4, chan // 2 % 2, chan % 2

    def tile(way, sign):
        ti = (i + sign * way[0] * (2 * oct_a - 1) + G) % G
        tj = (j + sign * way[1] * (2 * oct_b - 1) + G) % G
        tk = (k + sign * way[2] * (2 * oct_c - 1) + G) % G
        return (ti * G + tj) * G + tk

    def exists(way, sign):
        found = True
        for crosses, at, bit in zip(way, (i, j, k), (oct_a, oct_b, oct_c)):
            if crosses:
                to = at + sign * (2 * bit - 1)
                found = (to >= 0) & (to < G) & found
        return found

    gives = [exists(way, 1) for way, _, _ in PIECES]
    takes = [exists(way, -1) for way, _, _ in PIECES]

    def level(tile_at):
        return tile_at // 2 % 4

    later = [level(tile(way, 1)) > level(space) for way, _, _ in PIECES]
    earlier = [level(tile(way, -1)) < level(space) for way, _, _ in PIECES]
    barrier = pltpu.get_barrier_semaphore()
    for n in reversed(range(7)):

        @pl.when(takes[n] & ~earlier[n])
        def _():
            to = (tile(PIECES[n][0], -1), chan)
            pl.semaphore_signal(barrier, inc=1, device_id=to, device_id_type=MESH)

        @pl.when(gives[n] & later[n])
        def _():
            to = (tile(PIECES[n][0], 1), chan)
            pl.semaphore_signal(barrier, inc=1, device_id=to, device_id_type=MESH)

    for d in range(1, 8):
        pl.semaphore_signal(barrier, inc=1, device_id=(space, (chan + d) % 8), device_id_type=MESH)

    pairs = (x_hbm, x_ref), (p_hbm, pick), (q_hbm, pick_rim), (k1_hbm, k1), (k2_hbm, k2), (b1_hbm, b1_ref), (b2_hbm, b2_ref)
    loads = [
        pltpu.make_async_copy(src, dst, load_sem.at[n]) for n, (src, dst) in enumerate(pairs)
    ]
    for load in loads:
        load.start()

    r = lax.broadcasted_iota(jnp.int32, (RIM, OWN), 0)
    col = lax.broadcasted_iota(jnp.int32, (RIM, OWN), 1)
    xs, ys, zs = 32 * oct_a, 8 * oct_b, 2 * oct_c
    src = jnp.full((RIM, OWN), -1, jnp.int32)
    for way, start, rows in PIECES:
        q = r - (start - OWN)
        at = jnp.zeros_like(r)
        if way[2]:
            at = at + zs + (q & 1)
            q = q >> 1
        else:
            at = at + (q & 3)
            q = q >> 2
        if way[1]:
            at = at + ys + 4 * (q & 1)
            q = q >> 1
        else:
            at = at + 4 * (q & 3)
            q = q >> 2
        at = at + 16 * q + (xs if way[0] else 0)
        if way == (1, 1, 1):
            rows = 8
        inside = (r >= start - OWN) & (r < start - OWN + rows)
        src = jnp.where(inside, at, src)
    loads[0].wait()
    x = x_ref[...]
    select = jnp.where(src == col, 1.0, 0.0).astype(jnp.bfloat16)
    pack[...] = jnp.dot(select, x, preferred_element_type=jnp.float32).astype(jnp.bfloat16)
    land[chan, 0:OWN] = x

    for n, (_, start, rows) in enumerate(PIECES):

        @pl.when(~takes[n])
        def _():
            land[chan, start : start + rows] = jnp.zeros((rows, 128), jnp.bfloat16)

    greeted = [g & ~late for g, late in zip(gives, later)] + [t & early for t, early in zip(takes, earlier)]
    pl.semaphore_wait(barrier, 7 + sum(one.astype(jnp.int32) for one in greeted))
    for n in reversed(range(7)):

        @pl.when(takes[n] & earlier[n])
        def _():
            to = (tile(PIECES[n][0], -1), chan)
            pl.semaphore_signal(ready.at[n], inc=1, device_id=to, device_id_type=MESH)


    rims = []
    for n, (way, start, rows) in enumerate(PIECES):
        rims.append(
            pltpu.make_async_remote_copy(
                src_ref=pack.at[pl.ds(start - OWN, rows)],
                dst_ref=land.at[chan, pl.ds(start, rows)],
                send_sem=a_send.at[n],
                recv_sem=a_recv.at[n],
                device_id=(tile(way, 1), chan),
                device_id_type=MESH,
            )
        )
    for n in reversed(range(7)):
        pl.when(gives[n] & ~later[n])(rims[n].start)

    def to_tile(src_of, start, rows, send_sem, recv_sem):
        return [
            pltpu.make_async_remote_copy(
                src_ref=src_of,
                dst_ref=land.at[chan, pl.ds(start, rows)],
                send_sem=send_sem.at[d - 1],
                recv_sem=recv_sem.at[d - 1],
                device_id=(space, (chan + d) % 8),
                device_id_type=MESH,
            )
            for d in range(1, 8)
        ]

    owns = to_tile(x_ref, 0, OWN, b_send, b_recv)
    near = to_tile(land.at[chan, pl.ds(OWN, HALF)], OWN, HALF, c_send, c_recv)
    far = to_tile(land.at[chan, pl.ds(OWN + HALF, HALF)], OWN + HALF, HALF, d_send, d_recv)
    for copy in owns:
        copy.start()

    row = lax.broadcasted_iota(jnp.int32, (160, 256), 0)
    hy, hz = row >> 4, row & 15
    outside = ((j == 0) & (hy == 0)) | ((j == G - 1) & (hy == 9))
    outside = outside | ((k == 0) & (hz == 0)) | ((k == G - 1) & (hz == 9))
    mask[...] = jnp.where(outside, 0.0, 1.0).reshape(10, 16, 256)
    for load in loads[1:]:
        load.wait()
    for n in range(9):
        k2_t[n * 256 : (n + 1) * 256, :] = k2[n].T

    for n in range(NEAR):
        pl.when(takes[n])(rims[n].wait_recv)
    for copy in near:
        copy.start()
    for n in (0, 2, 3, 5, 4, 6):

        @pl.when(gives[n] & later[n])
        def _():
            pl.semaphore_wait(ready.at[n], 1)
            rims[n].start()

    for n in range(NEAR, 7):
        pl.when(takes[n])(rims[n].wait_recv)
    for copy in far:
        copy.start()
    for copy in owns:
        copy.wait_recv()
    for copy in near:
        copy.wait_recv()

    def unpack(matrix, chunks, x_of, y_of):
        sides = []
        for a in range(2):
            parts = []
            for s in range(4):
                for chunk in chunks:
                    parts.append(land[a * 4 + s, chunk : chunk + 16])
            sides.append(jnp.concatenate(parts, axis=0))
        voxels = jnp.concatenate(sides, axis=1)
        got = jnp.dot(matrix, voxels, preferred_element_type=jnp.float32).astype(jnp.bfloat16)
        rows = got.shape[0] // 3
        for a in range(2):
            for shift in range(3):
                piece = got[shift * rows : (shift + 1) * rows, a * 128 : (a + 1) * 128]
                piece = piece.reshape(rows // 16, 16, 128)
                at = 0
                for y, count in y_of:
                    wide[x_of[a], y : y + count, :, shift * 128 : (shift + 1) * 128] = piece[at : at + count]
                    at += count

    bias_one, bias_two = b1_ref[...], b2_ref[...]

    def stack(ref, at, planes, shift, y_of):
        parts = [ref[at : at + planes, y + shift : y + shift + count] for y, count in y_of]
        whole = jnp.concatenate(parts, axis=1) if len(parts) > 1 else parts[0]
        return whole.reshape(-1, whole.shape[3])

    def first(at, planes, y_of):
        taps = [stack(wide, at + a, planes, b, y_of) for a in range(3) for b in range(3)]
        total = jnp.dot(jnp.concatenate(taps, axis=1), k1[...], preferred_element_type=jnp.float32)
        total = jnp.maximum(total + bias_one, 0.0).reshape(planes, -1, 16, 256)
        for p in range(planes):
            inside = ((at + p > 0) | (i > 0)) & ((at + p < 9) | (i < G - 1))
            keep = jnp.where(inside, 1.0, 0.0)
            row = 0
            for y, count in y_of:
                plane = total[p, row : row + count] * (mask[y : y + count] * keep)
                hidden[at + p, y : y + count] = plane.astype(jnp.bfloat16)
                row += count

    def second(at, planes, y_of):
        taps = [stack(hidden, at + a, planes, b, y_of) for a in range(3) for b in range(3)]
        total = jnp.dot(jnp.concatenate(taps, axis=1), k2_t[...], preferred_element_type=jnp.float32)
        total = total.reshape(-1, 16, 96)
        result = total[:, 0:8, 0:32] + total[:, 1:9, 32:64] + total[:, 2:10, 64:96] + bias_two
        result = jnp.maximum(result, 0.0).astype(jnp.bfloat16).reshape(planes, -1, 8, 32)
        row = 0
        for y, count in y_of:
            out_ref[at : at + planes, y : y + count] = result[:, row : row + count]
            row += count

    def inner(p):
        for n in range(2):
            u = p + 2 * n
            unpack(pick[p], (16 * u, 64 + 16 * n), (2 + u, 6 + u), ((2, 8),))
        unpack(pick[p], (96 + 16 * p, 128), (10 + p, p), ((2, 8),))

    def outer(p):
        for n in range(2):
            u = p + 2 * n
            unpack(pick_rim[u], (144 + 16 * n, 176), (2 + u, 6 + u), ((0, 2), (10, 2)))
        unpack(pick_rim[p], (192, 208), (10 + p, p), ((0, 2), (10, 2)))

    inner(0)
    inner(1)
    first(0, 5, ((2, 6),))
    first(5, 5, ((2, 6),))
    second(0, 4, ((2, 4),))
    second(4, 4, ((2, 4),))

    for copy in far:
        copy.wait_recv()
    outer(0)
    outer(1)
    first(0, 5, ((0, 2), (8, 2)))
    first(5, 5, ((0, 2), (8, 2)))
    second(0, 4, ((0, 2), (6, 2)))
    second(4, 4, ((0, 2), (6, 2)))

    for n in range(7):
        pl.when(gives[n])(rims[n].wait_send)
    for copy in owns + near + far:
        copy.wait_send()


def on_device(blocks, kernel_one, bias_one, kernel_two, bias_two):
    cin, f1 = kernel_one.shape[3:]
    f2 = kernel_two.shape[4]
    vmem, hbm = pl.BlockSpec(memory_space=pltpu.VMEM), pl.BlockSpec(memory_space=pltpu.HBM)
    dma = pltpu.SemaphoreType.DMA
    out = pl.pallas_call(
        kernel,
        out_shape=jax.ShapeDtypeStruct((8, 8, 8, f2), jnp.bfloat16),
        in_specs=[hbm] * 7,
        out_specs=vmem,
        scratch_shapes=[
            pltpu.VMEM((OWN, cin), jnp.bfloat16),
            pltpu.VMEM((1, f1), jnp.float32),
            pltpu.VMEM((1, f2), jnp.float32),
            pltpu.VMEM((8, SLOT, cin), jnp.bfloat16),
            pltpu.VMEM((RIM, cin), jnp.bfloat16),
            pltpu.VMEM((27 * cin, f1), jnp.bfloat16),
            pltpu.VMEM((9, 3 * f2, f1), jnp.bfloat16),
            pltpu.VMEM((9 * f1, 3 * f2), jnp.bfloat16),
            pltpu.VMEM((2, 384, 128), jnp.bfloat16),
            pltpu.VMEM((4, 192, 128), jnp.bfloat16),
            pltpu.VMEM((12, 12, 16, 3 * cin), jnp.bfloat16),
            pltpu.VMEM((10, 10, 16, f1), jnp.bfloat16),
            pltpu.VMEM((10, 16, f1), jnp.float32),
            dma((7,)), dma((7,)), dma((7,)), dma((7,)), dma((7,)), dma((7,)), dma((7,)), dma((7,)), dma((7,)), pltpu.SemaphoreType.REGULAR((7,)),
        ],
        compiler_params=pltpu.CompilerParams(
            collective_id=0, has_side_effects=True, vmem_limit_bytes=64 * 1024 * 1024
        ),
        cost_estimate=pl.CostEstimate(flops=2_000_000_000, bytes_accessed=4_000_000, transcendentals=0),
    )(
        blocks.reshape(64, cin),
        kernel_one.reshape(27 * cin, f1),
        bias_one.reshape(1, f1),
        kernel_two.transpose(0, 1, 2, 4, 3).reshape(9, 3 * f2, f1),
        bias_two.reshape(1, f2),
        *(jnp.asarray(matrix) for matrix in unpack_matrices()),
    )
    return out.reshape(1, 8, 8, 8, f2)


def solution(mesh):
    placed = (
        P(("space", "chan"), None, None, None, None),
        P(),
        P(),
        P(None, None, None, None, "chan"),
        P("chan"),
    )
    return jax.shard_map(
        on_device,
        mesh=mesh,
        in_specs=placed,
        out_specs=P("space", None, None, None, "chan"),
        check_vma=False,
    )
```

```python
import jax
import jax.numpy as jnp
import numpy as np
from jax import lax
from jax.experimental import pallas as pl
from jax.experimental.pallas import tpu as pltpu
from jax.sharding import PartitionSpec as P

MESH = pl.DeviceIdType.MESH
G = 4
PIECES = (
    ((0, 0, 1), 64, 32),
    ((1, 0, 0), 96, 32),
    ((1, 0, 1), 128, 16),
    ((0, 1, 0), 144, 32),
    ((0, 1, 1), 176, 16),
    ((1, 1, 0), 192, 16),
    ((1, 1, 1), 208, 16),
)
NEAR = 3
OWN = 64
SLOT = 224
RIM = SLOT - OWN
HALF = RIM // 2


def unpack_matrices():
    def place(n):
        if n < 2:
            return 1, n
        return (1, n - 6) if n >= 6 and n < 10 else (0, (n - 2) % 8)

    inner = np.zeros((2, 3, 8, 16, 128), np.float32)
    outer = np.zeros((4, 3, 4, 16, 128), np.float32)
    for shift in range(3):
        for z in range(10):
            c, w = place(z + shift)
            rim = z + shift < 2 or z + shift >= 10
            for u in range(2):
                for y in range(8):
                    at = (2 * (y // 4) + c) * 32
                    v = y % 4
                    inner[u, shift, y, z, at + (16 + u * 8 + v * 2 + w if rim else v * 4 + w)] = 1
            for u in range(4):
                for y in range(4):
                    at = (2 * (1 - y // 2) + c) * 32
                    v = y % 2
                    outer[u, shift, y, z, at + (16 + u * 4 + v * 2 + w if rim else (u % 2) * 8 + v * 4 + w)] = 1
    return inner.reshape(2, 384, 128).astype(jnp.bfloat16), outer.reshape(4, 192, 128).astype(jnp.bfloat16)


def kernel(
    x_hbm, k1_hbm, b1_hbm, k2_hbm, b2_hbm, p_hbm, q_hbm, out_ref,
    x_ref, b1_ref, b2_ref, land, pack, k1, k2, k2_t, pick, pick_rim, wide, hidden, mask,
    load_sem, a_send, a_recv, b_send, b_recv, c_send, c_recv, d_send, d_recv, ready,
):
    space, chan = lax.axis_index("space"), lax.axis_index("chan")
    pairs = (x_hbm, x_ref), (p_hbm, pick), (q_hbm, pick_rim), (k1_hbm, k1), (k2_hbm, k2), (b1_hbm, b1_ref), (b2_hbm, b2_ref)
    loads = [
        pltpu.make_async_copy(src, dst, load_sem.at[n]) for n, (src, dst) in enumerate(pairs)
    ]
    for load in loads:
        load.start()

    i, j, k = space // (G * G), space // G % G, space % G
    oct_a, oct_b, oct_c = chan // 4, chan // 2 % 2, chan % 2

    def tile(way, sign):
        ti = (i + sign * way[0] * (2 * oct_a - 1) + G) % G
        tj = (j + sign * way[1] * (2 * oct_b - 1) + G) % G
        tk = (k + sign * way[2] * (2 * oct_c - 1) + G) % G
        return (ti * G + tj) * G + tk

    def exists(way, sign):
        found = True
        for crosses, at, bit in zip(way, (i, j, k), (oct_a, oct_b, oct_c)):
            if crosses:
                to = at + sign * (2 * bit - 1)
                found = (to >= 0) & (to < G) & found
        return found

    gives = [exists(way, 1) for way, _, _ in PIECES]
    takes = [exists(way, -1) for way, _, _ in PIECES]

    def level(tile_at):
        return tile_at // 2 % 4

    later = [level(tile(way, 1)) > level(space) for way, _, _ in PIECES]
    earlier = [level(tile(way, -1)) < level(space) for way, _, _ in PIECES]
    barrier = pltpu.get_barrier_semaphore()
    for n in reversed(range(7)):

        @pl.when(takes[n] & ~earlier[n])
        def _():
            to = (tile(PIECES[n][0], -1), chan)
            pl.semaphore_signal(barrier, inc=1, device_id=to, device_id_type=MESH)

        @pl.when(gives[n] & later[n])
        def _():
            to = (tile(PIECES[n][0], 1), chan)
            pl.semaphore_signal(barrier, inc=1, device_id=to, device_id_type=MESH)

    for d in range(1, 8):
        pl.semaphore_signal(barrier, inc=1, device_id=(space, (chan + d) % 8), device_id_type=MESH)

    r = lax.broadcasted_iota(jnp.int32, (RIM, OWN), 0)
    col = lax.broadcasted_iota(jnp.int32, (RIM, OWN), 1)
    xs, ys, zs = 32 * oct_a, 8 * oct_b, 2 * oct_c
    src = jnp.full((RIM, OWN), -1, jnp.int32)
    for way, start, rows in PIECES:
        q = r - (start - OWN)
        at = jnp.zeros_like(r)
        if way[2]:
            at = at + zs + (q & 1)
            q = q >> 1
        else:
            at = at + (q & 3)
            q = q >> 2
        if way[1]:
            at = at + ys + 4 * (q & 1)
            q = q >> 1
        else:
            at = at + 4 * (q & 3)
            q = q >> 2
        at = at + 16 * q + (xs if way[0] else 0)
        if way == (1, 1, 1):
            rows = 8
        inside = (r >= start - OWN) & (r < start - OWN + rows)
        src = jnp.where(inside, at, src)
    loads[0].wait()
    x = x_ref[...]
    select = jnp.where(src == col, 1.0, 0.0).astype(jnp.bfloat16)
    pack[...] = jnp.dot(select, x, preferred_element_type=jnp.float32).astype(jnp.bfloat16)
    land[chan, 0:OWN] = x

    for n, (_, start, rows) in enumerate(PIECES):

        @pl.when(~takes[n])
        def _():
            land[chan, start : start + rows] = jnp.zeros((rows, 128), jnp.bfloat16)

    greeted = [g & ~late for g, late in zip(gives, later)] + [t & early for t, early in zip(takes, earlier)]
    pl.semaphore_wait(barrier, 7 + sum(one.astype(jnp.int32) for one in greeted))
    for n in reversed(range(7)):

        @pl.when(takes[n] & earlier[n])
        def _():
            to = (tile(PIECES[n][0], -1), chan)
            pl.semaphore_signal(ready.at[n], inc=1, device_id=to, device_id_type=MESH)


    rims = []
    for n, (way, start, rows) in enumerate(PIECES):
        rims.append(
            pltpu.make_async_remote_copy(
                src_ref=pack.at[pl.ds(start - OWN, rows)],
                dst_ref=land.at[chan, pl.ds(start, rows)],
                send_sem=a_send.at[n],
                recv_sem=a_recv.at[n],
                device_id=(tile(way, 1), chan),
                device_id_type=MESH,
            )
        )
    for n in reversed(range(7)):
        pl.when(gives[n] & ~later[n])(rims[n].start)

    def to_tile(src_of, start, rows, send_sem, recv_sem):
        return [
            pltpu.make_async_remote_copy(
                src_ref=src_of,
                dst_ref=land.at[chan, pl.ds(start, rows)],
                send_sem=send_sem.at[d - 1],
                recv_sem=recv_sem.at[d - 1],
                device_id=(space, (chan + d) % 8),
                device_id_type=MESH,
            )
            for d in range(1, 8)
        ]

    owns = to_tile(x_ref, 0, OWN, b_send, b_recv)
    near = to_tile(land.at[chan, pl.ds(OWN, HALF)], OWN, HALF, c_send, c_recv)
    far = to_tile(land.at[chan, pl.ds(OWN + HALF, HALF)], OWN + HALF, HALF, d_send, d_recv)
    for copy in owns:
        copy.start()

    for n in range(NEAR):

        @pl.when(gives[n] & later[n])
        def _():
            pl.semaphore_wait(ready.at[n], 1)
            rims[n].start()

    row = lax.broadcasted_iota(jnp.int32, (160, 256), 0)
    hy, hz = row >> 4, row & 15
    outside = ((j == 0) & (hy == 0)) | ((j == G - 1) & (hy == 9))
    outside = outside | ((k == 0) & (hz == 0)) | ((k == G - 1) & (hz == 9))
    mask[...] = jnp.where(outside, 0.0, 1.0).reshape(10, 16, 256)
    for load in loads[1:]:
        load.wait()
    for n in range(9):
        k2_t[n * 256 : (n + 1) * 256, :] = k2[n].T

    for n in range(NEAR):
        pl.when(takes[n])(rims[n].wait_recv)
    for copy in near:
        copy.start()
    for n in (3, 5, 4, 6):

        @pl.when(gives[n] & later[n])
        def _():
            pl.semaphore_wait(ready.at[n], 1)
            rims[n].start()

    for n in range(NEAR, 7):
        pl.when(takes[n])(rims[n].wait_recv)
    for copy in far:
        copy.start()
    for copy in owns:
        copy.wait_recv()
    for copy in near:
        copy.wait_recv()

    def unpack(matrix, chunks, x_of, y_of):
        sides = []
        for a in range(2):
            parts = []
            for s in range(4):
                for chunk in chunks:
                    parts.append(land[a * 4 + s, chunk : chunk + 16])
            sides.append(jnp.concatenate(parts, axis=0))
        voxels = jnp.concatenate(sides, axis=1)
        got = jnp.dot(matrix, voxels, preferred_element_type=jnp.float32).astype(jnp.bfloat16)
        rows = got.shape[0] // 3
        for a in range(2):
            for shift in range(3):
                piece = got[shift * rows : (shift + 1) * rows, a * 128 : (a + 1) * 128]
                piece = piece.reshape(rows // 16, 16, 128)
                at = 0
                for y, count in y_of:
                    wide[x_of[a], y : y + count, :, shift * 128 : (shift + 1) * 128] = piece[at : at + count]
                    at += count

    bias_one, bias_two = b1_ref[...], b2_ref[...]

    def stack(ref, at, planes, shift, y_of):
        parts = [ref[at : at + planes, y + shift : y + shift + count] for y, count in y_of]
        whole = jnp.concatenate(parts, axis=1) if len(parts) > 1 else parts[0]
        return whole.reshape(-1, whole.shape[3])

    def first(at, planes, y_of):
        taps = [stack(wide, at + a, planes, b, y_of) for a in range(3) for b in range(3)]
        total = jnp.dot(jnp.concatenate(taps, axis=1), k1[...], preferred_element_type=jnp.float32)
        total = jnp.maximum(total + bias_one, 0.0).reshape(planes, -1, 16, 256)
        for p in range(planes):
            inside = ((at + p > 0) | (i > 0)) & ((at + p < 9) | (i < G - 1))
            keep = jnp.where(inside, 1.0, 0.0)
            row = 0
            for y, count in y_of:
                plane = total[p, row : row + count] * (mask[y : y + count] * keep)
                hidden[at + p, y : y + count] = plane.astype(jnp.bfloat16)
                row += count

    def second(at, planes, y_of):
        taps = [stack(hidden, at + a, planes, b, y_of) for a in range(3) for b in range(3)]
        total = jnp.dot(jnp.concatenate(taps, axis=1), k2_t[...], preferred_element_type=jnp.float32)
        total = total.reshape(-1, 16, 96)
        result = total[:, 0:8, 0:32] + total[:, 1:9, 32:64] + total[:, 2:10, 64:96] + bias_two
        result = jnp.maximum(result, 0.0).astype(jnp.bfloat16).reshape(planes, -1, 8, 32)
        row = 0
        for y, count in y_of:
            out_ref[at : at + planes, y : y + count] = result[:, row : row + count]
            row += count

    def inner(p):
        for n in range(2):
            u = p + 2 * n
            unpack(pick[p], (16 * u, 64 + 16 * n), (2 + u, 6 + u), ((2, 8),))
        unpack(pick[p], (96 + 16 * p, 128), (10 + p, p), ((2, 8),))

    def outer(p):
        for n in range(2):
            u = p + 2 * n
            unpack(pick_rim[u], (144 + 16 * n, 176), (2 + u, 6 + u), ((0, 2), (10, 2)))
        unpack(pick_rim[p], (192, 208), (10 + p, p), ((0, 2), (10, 2)))

    inner(0)
    inner(1)
    first(0, 5, ((2, 6),))
    first(5, 5, ((2, 6),))
    second(0, 4, ((2, 4),))
    second(4, 4, ((2, 4),))

    for copy in far:
        copy.wait_recv()
    outer(0)
    outer(1)
    first(0, 5, ((0, 2), (8, 2)))
    first(5, 5, ((0, 2), (8, 2)))
    second(0, 4, ((0, 2), (6, 2)))
    second(4, 4, ((0, 2), (6, 2)))

    for n in range(7):
        pl.when(gives[n])(rims[n].wait_send)
    for copy in owns + near + far:
        copy.wait_send()


def on_device(blocks, kernel_one, bias_one, kernel_two, bias_two):
    cin, f1 = kernel_one.shape[3:]
    f2 = kernel_two.shape[4]
    vmem, hbm = pl.BlockSpec(memory_space=pltpu.VMEM), pl.BlockSpec(memory_space=pltpu.HBM)
    dma = pltpu.SemaphoreType.DMA
    out = pl.pallas_call(
        kernel,
        out_shape=jax.ShapeDtypeStruct((8, 8, 8, f2), jnp.bfloat16),
        in_specs=[hbm] * 7,
        out_specs=vmem,
        scratch_shapes=[
            pltpu.VMEM((OWN, cin), jnp.bfloat16),
            pltpu.VMEM((1, f1), jnp.float32),
            pltpu.VMEM((1, f2), jnp.float32),
            pltpu.VMEM((8, SLOT, cin), jnp.bfloat16),
            pltpu.VMEM((RIM, cin), jnp.bfloat16),
            pltpu.VMEM((27 * cin, f1), jnp.bfloat16),
            pltpu.VMEM((9, 3 * f2, f1), jnp.bfloat16),
            pltpu.VMEM((9 * f1, 3 * f2), jnp.bfloat16),
            pltpu.VMEM((2, 384, 128), jnp.bfloat16),
            pltpu.VMEM((4, 192, 128), jnp.bfloat16),
            pltpu.VMEM((12, 12, 16, 3 * cin), jnp.bfloat16),
            pltpu.VMEM((10, 10, 16, f1), jnp.bfloat16),
            pltpu.VMEM((10, 16, f1), jnp.float32),
            dma((7,)), dma((7,)), dma((7,)), dma((7,)), dma((7,)), dma((7,)), dma((7,)), dma((7,)), dma((7,)), pltpu.SemaphoreType.REGULAR((7,)),
        ],
        compiler_params=pltpu.CompilerParams(
            collective_id=0, has_side_effects=True, vmem_limit_bytes=64 * 1024 * 1024
        ),
        cost_estimate=pl.CostEstimate(flops=2_000_000_000, bytes_accessed=4_000_000, transcendentals=0),
    )(
        blocks.reshape(64, cin),
        kernel_one.reshape(27 * cin, f1),
        bias_one.reshape(1, f1),
        kernel_two.transpose(0, 1, 2, 4, 3).reshape(9, 3 * f2, f1),
        bias_two.reshape(1, f2),
        *(jnp.asarray(matrix) for matrix in unpack_matrices()),
    )
    return out.reshape(1, 8, 8, 8, f2)


def solution(mesh):
    placed = (
        P(("space", "chan"), None, None, None, None),
        P(),
        P(),
        P(None, None, None, None, "chan"),
        P("chan"),
    )
    return jax.shard_map(
        on_device,
        mesh=mesh,
        in_specs=placed,
        out_specs=P("space", None, None, None, "chan"),
        check_vma=False,
    )
```

```python
import jax
import jax.numpy as jnp
import numpy as np
from jax import lax
from jax.experimental import pallas as pl
from jax.experimental.pallas import tpu as pltpu
from jax.sharding import PartitionSpec as P

MESH = pl.DeviceIdType.MESH
G = 4
PIECES = (
    ((0, 0, 1), 64, 32),
    ((1, 0, 0), 96, 32),
    ((1, 0, 1), 128, 16),
    ((0, 1, 0), 144, 32),
    ((0, 1, 1), 176, 16),
    ((1, 1, 0), 192, 16),
    ((1, 1, 1), 208, 16),
)
NEAR = 3
OWN = 64
SLOT = 224
RIM = SLOT - OWN
HALF = RIM // 2


def unpack_matrices():
    def place(n):
        if n < 2:
            return 1, n
        return (1, n - 6) if n >= 6 and n < 10 else (0, (n - 2) % 8)

    inner = np.zeros((2, 3, 8, 16, 128), np.float32)
    outer = np.zeros((4, 3, 4, 16, 128), np.float32)
    for shift in range(3):
        for z in range(10):
            c, w = place(z + shift)
            rim = z + shift < 2 or z + shift >= 10
            for u in range(2):
                for y in range(8):
                    at = (2 * (y // 4) + c) * 32
                    v = y % 4
                    inner[u, shift, y, z, at + (16 + u * 8 + v * 2 + w if rim else v * 4 + w)] = 1
            for u in range(4):
                for y in range(4):
                    at = (2 * (1 - y // 2) + c) * 32
                    v = y % 2
                    outer[u, shift, y, z, at + (16 + u * 4 + v * 2 + w if rim else (u % 2) * 8 + v * 4 + w)] = 1
    return inner.reshape(2, 384, 128).astype(jnp.bfloat16), outer.reshape(4, 192, 128).astype(jnp.bfloat16)


def kernel(
    x_hbm, k1_hbm, b1_hbm, k2_hbm, b2_hbm, p_hbm, q_hbm, out_ref,
    x_ref, b1_ref, b2_ref, land, pack, k1, k2, k2_t, pick, pick_rim, wide, hidden, mask,
    load_sem, a_send, a_recv, b_send, b_recv, c_send, c_recv, d_send, d_recv, ready,
):
    space, chan = lax.axis_index("space"), lax.axis_index("chan")
    pairs = (x_hbm, x_ref), (p_hbm, pick), (q_hbm, pick_rim), (k1_hbm, k1), (k2_hbm, k2), (b1_hbm, b1_ref), (b2_hbm, b2_ref)
    loads = [
        pltpu.make_async_copy(src, dst, load_sem.at[n]) for n, (src, dst) in enumerate(pairs)
    ]
    for load in loads:
        load.start()

    i, j, k = space // (G * G), space // G % G, space % G
    oct_a, oct_b, oct_c = chan // 4, chan // 2 % 2, chan % 2

    def tile(way, sign):
        ti = (i + sign * way[0] * (2 * oct_a - 1) + G) % G
        tj = (j + sign * way[1] * (2 * oct_b - 1) + G) % G
        tk = (k + sign * way[2] * (2 * oct_c - 1) + G) % G
        return (ti * G + tj) * G + tk

    def exists(way, sign):
        found = True
        for crosses, at, bit in zip(way, (i, j, k), (oct_a, oct_b, oct_c)):
            if crosses:
                to = at + sign * (2 * bit - 1)
                found = (to >= 0) & (to < G) & found
        return found

    gives = [exists(way, 1) for way, _, _ in PIECES]
    takes = [exists(way, -1) for way, _, _ in PIECES]

    def level(tile_at):
        y = tile_at // 16
        return 4 * (tile_at // 2 % 4) + y + (y == 2) - (y == 3)

    later = [level(tile(way, 1)) > level(space) for way, _, _ in PIECES]
    earlier = [level(tile(way, -1)) < level(space) for way, _, _ in PIECES]
    barrier = pltpu.get_barrier_semaphore()
    for n in reversed(range(7)):

        @pl.when(takes[n] & ~earlier[n])
        def _():
            to = (tile(PIECES[n][0], -1), chan)
            pl.semaphore_signal(barrier, inc=1, device_id=to, device_id_type=MESH)

        @pl.when(gives[n] & later[n])
        def _():
            to = (tile(PIECES[n][0], 1), chan)
            pl.semaphore_signal(barrier, inc=1, device_id=to, device_id_type=MESH)

    for d in range(1, 8):
        pl.semaphore_signal(barrier, inc=1, device_id=(space, (chan + d) % 8), device_id_type=MESH)

    r = lax.broadcasted_iota(jnp.int32, (RIM, OWN), 0)
    col = lax.broadcasted_iota(jnp.int32, (RIM, OWN), 1)
    xs, ys, zs = 32 * oct_a, 8 * oct_b, 2 * oct_c
    src = jnp.full((RIM, OWN), -1, jnp.int32)
    for way, start, rows in PIECES:
        q = r - (start - OWN)
        at = jnp.zeros_like(r)
        if way[2]:
            at = at + zs + (q & 1)
            q = q >> 1
        else:
            at = at + (q & 3)
            q = q >> 2
        if way[1]:
            at = at + ys + 4 * (q & 1)
            q = q >> 1
        else:
            at = at + 4 * (q & 3)
            q = q >> 2
        at = at + 16 * q + (xs if way[0] else 0)
        if way == (1, 1, 1):
            rows = 8
        inside = (r >= start - OWN) & (r < start - OWN + rows)
        src = jnp.where(inside, at, src)
    loads[0].wait()
    x = x_ref[...]
    select = jnp.where(src == col, 1.0, 0.0).astype(jnp.bfloat16)
    pack[...] = jnp.dot(select, x, preferred_element_type=jnp.float32).astype(jnp.bfloat16)
    land[chan, 0:OWN] = x

    for n, (_, start, rows) in enumerate(PIECES):

        @pl.when(~takes[n])
        def _():
            land[chan, start : start + rows] = jnp.zeros((rows, 128), jnp.bfloat16)

    greeted = [g & ~late for g, late in zip(gives, later)] + [t & early for t, early in zip(takes, earlier)]
    pl.semaphore_wait(barrier, 7 + sum(one.astype(jnp.int32) for one in greeted))
    for n in reversed(range(7)):

        @pl.when(takes[n] & earlier[n])
        def _():
            to = (tile(PIECES[n][0], -1), chan)
            pl.semaphore_signal(ready.at[n], inc=1, device_id=to, device_id_type=MESH)


    rims = []
    for n, (way, start, rows) in enumerate(PIECES):
        rims.append(
            pltpu.make_async_remote_copy(
                src_ref=pack.at[pl.ds(start - OWN, rows)],
                dst_ref=land.at[chan, pl.ds(start, rows)],
                send_sem=a_send.at[n],
                recv_sem=a_recv.at[n],
                device_id=(tile(way, 1), chan),
                device_id_type=MESH,
            )
        )
    for n in reversed(range(7)):
        pl.when(gives[n] & ~later[n])(rims[n].start)

    def to_tile(src_of, start, rows, send_sem, recv_sem):
        return [
            pltpu.make_async_remote_copy(
                src_ref=src_of,
                dst_ref=land.at[chan, pl.ds(start, rows)],
                send_sem=send_sem.at[d - 1],
                recv_sem=recv_sem.at[d - 1],
                device_id=(space, (chan + d) % 8),
                device_id_type=MESH,
            )
            for d in range(1, 8)
        ]

    owns = to_tile(x_ref, 0, OWN, b_send, b_recv)
    near = to_tile(land.at[chan, pl.ds(OWN, HALF)], OWN, HALF, c_send, c_recv)
    far = to_tile(land.at[chan, pl.ds(OWN + HALF, HALF)], OWN + HALF, HALF, d_send, d_recv)
    for copy in owns:
        copy.start()

    for n in range(NEAR):

        @pl.when(gives[n] & later[n])
        def _():
            pl.semaphore_wait(ready.at[n], 1)
            rims[n].start()

    row = lax.broadcasted_iota(jnp.int32, (160, 256), 0)
    hy, hz = row >> 4, row & 15
    outside = ((j == 0) & (hy == 0)) | ((j == G - 1) & (hy == 9))
    outside = outside | ((k == 0) & (hz == 0)) | ((k == G - 1) & (hz == 9))
    mask[...] = jnp.where(outside, 0.0, 1.0).reshape(10, 16, 256)
    for load in loads[1:]:
        load.wait()
    for n in range(9):
        k2_t[n * 256 : (n + 1) * 256, :] = k2[n].T

    for n in range(NEAR):
        pl.when(takes[n])(rims[n].wait_recv)
    for copy in near:
        copy.start()
    for n in (3, 5, 4, 6):

        @pl.when(gives[n] & later[n])
        def _():
            pl.semaphore_wait(ready.at[n], 1)
            rims[n].start()

    for n in range(NEAR, 7):
        pl.when(takes[n])(rims[n].wait_recv)
    for copy in far:
        copy.start()
    for copy in owns:
        copy.wait_recv()
    for copy in near:
        copy.wait_recv()

    def unpack(matrix, chunks, x_of, y_of):
        sides = []
        for a in range(2):
            parts = []
            for s in range(4):
                for chunk in chunks:
                    parts.append(land[a * 4 + s, chunk : chunk + 16])
            sides.append(jnp.concatenate(parts, axis=0))
        voxels = jnp.concatenate(sides, axis=1)
        got = jnp.dot(matrix, voxels, preferred_element_type=jnp.float32).astype(jnp.bfloat16)
        rows = got.shape[0] // 3
        for a in range(2):
            for shift in range(3):
                piece = got[shift * rows : (shift + 1) * rows, a * 128 : (a + 1) * 128]
                piece = piece.reshape(rows // 16, 16, 128)
                at = 0
                for y, count in y_of:
                    wide[x_of[a], y : y + count, :, shift * 128 : (shift + 1) * 128] = piece[at : at + count]
                    at += count

    bias_one, bias_two = b1_ref[...], b2_ref[...]

    def stack(ref, at, planes, shift, y_of):
        parts = [ref[at : at + planes, y + shift : y + shift + count] for y, count in y_of]
        whole = jnp.concatenate(parts, axis=1) if len(parts) > 1 else parts[0]
        return whole.reshape(-1, whole.shape[3])

    def first(at, planes, y_of):
        taps = [stack(wide, at + a, planes, b, y_of) for a in range(3) for b in range(3)]
        total = jnp.dot(jnp.concatenate(taps, axis=1), k1[...], preferred_element_type=jnp.float32)
        total = jnp.maximum(total + bias_one, 0.0).reshape(planes, -1, 16, 256)
        for p in range(planes):
            inside = ((at + p > 0) | (i > 0)) & ((at + p < 9) | (i < G - 1))
            keep = jnp.where(inside, 1.0, 0.0)
            row = 0
            for y, count in y_of:
                plane = total[p, row : row + count] * (mask[y : y + count] * keep)
                hidden[at + p, y : y + count] = plane.astype(jnp.bfloat16)
                row += count

    def second(at, planes, y_of):
        taps = [stack(hidden, at + a, planes, b, y_of) for a in range(3) for b in range(3)]
        total = jnp.dot(jnp.concatenate(taps, axis=1), k2_t[...], preferred_element_type=jnp.float32)
        total = total.reshape(-1, 16, 96)
        result = total[:, 0:8, 0:32] + total[:, 1:9, 32:64] + total[:, 2:10, 64:96] + bias_two
        result = jnp.maximum(result, 0.0).astype(jnp.bfloat16).reshape(planes, -1, 8, 32)
        row = 0
        for y, count in y_of:
            out_ref[at : at + planes, y : y + count] = result[:, row : row + count]
            row += count

    def inner(p):
        for n in range(2):
            u = p + 2 * n
            unpack(pick[p], (16 * u, 64 + 16 * n), (2 + u, 6 + u), ((2, 8),))
        unpack(pick[p], (96 + 16 * p, 128), (10 + p, p), ((2, 8),))

    def outer(p):
        for n in range(2):
            u = p + 2 * n
            unpack(pick_rim[u], (144 + 16 * n, 176), (2 + u, 6 + u), ((0, 2), (10, 2)))
        unpack(pick_rim[p], (192, 208), (10 + p, p), ((0, 2), (10, 2)))

    inner(0)
    inner(1)
    first(0, 5, ((2, 6),))
    first(5, 5, ((2, 6),))
    second(0, 4, ((2, 4),))
    second(4, 4, ((2, 4),))

    for copy in far:
        copy.wait_recv()
    outer(0)
    outer(1)
    first(0, 5, ((0, 2), (8, 2)))
    first(5, 5, ((0, 2), (8, 2)))
    second(0, 4, ((0, 2), (6, 2)))
    second(4, 4, ((0, 2), (6, 2)))

    for n in range(7):
        pl.when(gives[n])(rims[n].wait_send)
    for copy in owns + near + far:
        copy.wait_send()


def on_device(blocks, kernel_one, bias_one, kernel_two, bias_two):
    cin, f1 = kernel_one.shape[3:]
    f2 = kernel_two.shape[4]
    vmem, hbm = pl.BlockSpec(memory_space=pltpu.VMEM), pl.BlockSpec(memory_space=pltpu.HBM)
    dma = pltpu.SemaphoreType.DMA
    out = pl.pallas_call(
        kernel,
        out_shape=jax.ShapeDtypeStruct((8, 8, 8, f2), jnp.bfloat16),
        in_specs=[hbm] * 7,
        out_specs=vmem,
        scratch_shapes=[
            pltpu.VMEM((OWN, cin), jnp.bfloat16),
            pltpu.VMEM((1, f1), jnp.float32),
            pltpu.VMEM((1, f2), jnp.float32),
            pltpu.VMEM((8, SLOT, cin), jnp.bfloat16),
            pltpu.VMEM((RIM, cin), jnp.bfloat16),
            pltpu.VMEM((27 * cin, f1), jnp.bfloat16),
            pltpu.VMEM((9, 3 * f2, f1), jnp.bfloat16),
            pltpu.VMEM((9 * f1, 3 * f2), jnp.bfloat16),
            pltpu.VMEM((2, 384, 128), jnp.bfloat16),
            pltpu.VMEM((4, 192, 128), jnp.bfloat16),
            pltpu.VMEM((12, 12, 16, 3 * cin), jnp.bfloat16),
            pltpu.VMEM((10, 10, 16, f1), jnp.bfloat16),
            pltpu.VMEM((10, 16, f1), jnp.float32),
            dma((7,)), dma((7,)), dma((7,)), dma((7,)), dma((7,)), dma((7,)), dma((7,)), dma((7,)), dma((7,)), pltpu.SemaphoreType.REGULAR((7,)),
        ],
        compiler_params=pltpu.CompilerParams(
            collective_id=0, has_side_effects=True, vmem_limit_bytes=64 * 1024 * 1024
        ),
        cost_estimate=pl.CostEstimate(flops=2_000_000_000, bytes_accessed=4_000_000, transcendentals=0),
    )(
        blocks.reshape(64, cin),
        kernel_one.reshape(27 * cin, f1),
        bias_one.reshape(1, f1),
        kernel_two.transpose(0, 1, 2, 4, 3).reshape(9, 3 * f2, f1),
        bias_two.reshape(1, f2),
        *(jnp.asarray(matrix) for matrix in unpack_matrices()),
    )
    return out.reshape(1, 8, 8, 8, f2)


def solution(mesh):
    placed = (
        P(("space", "chan"), None, None, None, None),
        P(),
        P(),
        P(None, None, None, None, "chan"),
        P("chan"),
    )
    return jax.shard_map(
        on_device,
        mesh=mesh,
        in_specs=placed,
        out_specs=P("space", None, None, None, "chan"),
        check_vma=False,
    )
```
